32 devices in a mesh: seq: 16 (over z, y, x), head: 2 (over core).
Axes of the slice: x: 2, y: 2, z: 4, core: 2. Of those that a mesh axis runs over, the one named last changes fastest.
Arguments:
- queries: bfloat16 [4096, 2048], P('seq', 'head'), may hold values from -4 to 4
- first_pair_keys: bfloat16 [4096, 1024], P('seq', 'head'), may hold values from -4 to 4
- first_pair_values: bfloat16 [4096, 1024], P('seq', 'head'), may hold values from -6 to 6
- second_pair_keys: bfloat16 [4096, 1024], P('seq', 'head'), may hold values from -4 to 4
- second_pair_values: bfloat16 [4096, 1024], P('seq', 'head'), may hold values from -6 to 6
- out_weight: bfloat16 [2048, 8192], P('seq', 'head'), may hold values from -0.125 to 0.125
Outputs:
- attended: bfloat16 [4096, 2048], P('seq', 'head')
- projected: bfloat16 [4096, 8192], P('seq', 'head')
The draws below stay inside these ranges and needn't reach their ends.
All inputs are finite; a program needn't handle non-finite values.
Results may differ from the reference program's by a relative error of at most 0.0064.
Values may be sent and summed in bfloat16 or wider, within the bound.
A program may use at most 192 MiB of HBM per device.

```python
import math
import jax
import jax.numpy as jnp
from jax import lax

HEAD_SIZE = 128
KEY_VALUE_HEADS = 8
GROUP_QUERIES = 2
HQ = 16
DM = 8192
FIRST_WINDOW = 512
SECOND_WINDOW = 32
SEQUENCE_TOKENS = 4096


def backdrop_fill(key, salt, shape):
    subkey = jax.random.fold_in(key, salt)
    return jnp.clip(jax.random.normal(subkey, shape, jnp.float32), -4.0, 4.0)


def draw_queries(key, part):
    value_entries = backdrop_fill(key, 11, (SEQUENCE_TOKENS, KEY_VALUE_HEADS, GROUP_QUERIES, HEAD_SIZE))
    return value_entries.reshape(SEQUENCE_TOKENS, KEY_VALUE_HEADS * GROUP_QUERIES * HEAD_SIZE).astype(jnp.bfloat16)


def draw_first_pair_keys(key, part):
    value_entries = backdrop_fill(key, 12, (SEQUENCE_TOKENS, KEY_VALUE_HEADS, HEAD_SIZE))
    return value_entries.reshape(SEQUENCE_TOKENS, KEY_VALUE_HEADS * HEAD_SIZE).astype(jnp.bfloat16)


def draw_second_pair_keys(key, part):
    value_entries = backdrop_fill(key, 13, (SEQUENCE_TOKENS, KEY_VALUE_HEADS, HEAD_SIZE))
    return value_entries.reshape(SEQUENCE_TOKENS, KEY_VALUE_HEADS * HEAD_SIZE).astype(jnp.bfloat16)


def block_levels(key, shape, shards, least, largest):
    factor_of, own = 1.0, jax.random.fold_in(key, 6)
    for axis_at, shards_of in shards:
        draws = jnp.exp(jax.random.uniform(jax.random.fold_in(own, axis_at), (shards_of,), jnp.float32, least / len(shards), largest / len(shards)))
        factor_of = factor_of * jnp.repeat(draws, shape[axis_at] // shards_of).reshape([-1 if axis == axis_at else 1 for axis in range(len(shape))])
    return factor_of


def noise(rng, dims, scale, limit, shards=(), kind=jnp.bfloat16):
    entries = jax.random.normal(rng, dims, jnp.float32) * scale
    if len(shards) > 0:
        entries = block_levels(rng, dims, shards, -0.22, 0.18) * entries
    return jnp.clip(entries, min=-limit, max=limit).astype(kind)


def setup_inputs(seed: int = 0) -> dict:
    keys = jax.random.split(jax.random.key(seed), 7)
    return {
        "queries": draw_queries(jax.random.fold_in(keys[6], 71), 0),
        "first_pair_keys": draw_first_pair_keys(jax.random.fold_in(keys[6], 71), 0),
        "first_pair_values": noise(keys[2], (SEQUENCE_TOKENS, KEY_VALUE_HEADS * HEAD_SIZE), 1.0, 6.0, ((0, 16), (1, 2))),
        "second_pair_keys": draw_second_pair_keys(jax.random.fold_in(keys[6], 71), 0),
        "second_pair_values": noise(keys[4], (SEQUENCE_TOKENS, KEY_VALUE_HEADS * HEAD_SIZE), 1.0, 6.0, ((0, 16), (1, 2))),
        "out_weight": noise(keys[5], (HQ * HEAD_SIZE, DM), (HQ * HEAD_SIZE) ** -0.5, 0.125, ((0, 16), (1, 2))),
    }


def attend_block(query_rows, first_rows, first_vals, second_win, second_vwin, query_pos, key_pos):
    score_scale = HEAD_SIZE ** -0.5
    query_mod = (query_rows.astype(jnp.float32)[:, None] * second_win.astype(jnp.float32)[:, :, :, None, :]).astype(jnp.bfloat16)
    scores = jnp.einsum("itvgd,jvd->ivgtj", query_mod.astype(jnp.float32), first_rows.astype(jnp.float32)) * score_scale
    key_lag = query_pos[:, None] - key_pos[None, :]
    first_ok = (key_lag >= 0) & (key_lag < FIRST_WINDOW) & (key_pos[None, :] >= 0)
    offsets = jnp.arange(SECOND_WINDOW, dtype=jnp.int32)
    second_ok = (query_pos[:, None] - offsets[None, :]) >= 0
    is_valid = first_ok[:, None, None, None, :] & second_ok[:, None, None, :, None]
    scores = jnp.where(is_valid, scores, -jnp.inf)
    row_top = jnp.max(scores, axis=(3, 4), keepdims=True)
    row_weights = jnp.exp(scores - row_top)
    row_sum = jnp.sum(row_weights, axis=(3, 4))
    weights_bf = row_weights.astype(jnp.bfloat16)
    first_mix = jnp.einsum("ivgtj,jvd->ivgtd", weights_bf.astype(jnp.float32), first_vals.astype(jnp.float32))
    second_side = jnp.transpose(second_vwin, (0, 2, 1, 3)).astype(jnp.float32)[:, :, None]
    combined = jnp.sum(first_mix * second_side, axis=3)
    return (combined / row_sum[..., None]).astype(jnp.bfloat16)


def reference(queries, first_pair_keys, first_pair_values, second_pair_keys, second_pair_values, out_weight):
    token_count = queries.shape[0]
    block_rows = math.gcd(128, token_count)
    query_head_count = queries.reshape(token_count, KEY_VALUE_HEADS, GROUP_QUERIES, HEAD_SIZE)
    leading_first = jnp.zeros((FIRST_WINDOW, KEY_VALUE_HEADS, HEAD_SIZE), jnp.bfloat16)
    leading_second = jnp.zeros((SECOND_WINDOW - 1, KEY_VALUE_HEADS, HEAD_SIZE), jnp.bfloat16)
    padded_first_keys = jnp.concatenate([leading_first, first_pair_keys.reshape(token_count, KEY_VALUE_HEADS, HEAD_SIZE)], axis=0)
    padded_first_values = jnp.concatenate([leading_first, first_pair_values.reshape(token_count, KEY_VALUE_HEADS, HEAD_SIZE)], axis=0)
    padded_second_keys = jnp.concatenate([leading_second, second_pair_keys.reshape(token_count, KEY_VALUE_HEADS, HEAD_SIZE)], axis=0)
    padded_second_values = jnp.concatenate([leading_second, second_pair_values.reshape(token_count, KEY_VALUE_HEADS, HEAD_SIZE)], axis=0)

    def one_block(block_index):
        block_start = (block_index * block_rows).astype(jnp.int32)
        query_rows = lax.dynamic_slice_in_dim(query_head_count, block_start, block_rows, 0)
        first_rows = lax.dynamic_slice_in_dim(padded_first_keys, block_start, block_rows + FIRST_WINDOW, 0)
        first_vals = lax.dynamic_slice_in_dim(padded_first_values, block_start, block_rows + FIRST_WINDOW, 0)
        near_keys = lax.dynamic_slice_in_dim(padded_second_keys, block_start, block_rows + SECOND_WINDOW - 1, 0)
        near_vals = lax.dynamic_slice_in_dim(padded_second_values, block_start, block_rows + SECOND_WINDOW - 1, 0)
        second_win = jnp.stack([near_keys[SECOND_WINDOW - 1 - lag_step: SECOND_WINDOW - 1 - lag_step + block_rows] for lag_step in range(SECOND_WINDOW)], axis=1)
        second_vwin = jnp.stack([near_vals[SECOND_WINDOW - 1 - lag_step: SECOND_WINDOW - 1 - lag_step + block_rows] for lag_step in range(SECOND_WINDOW)], axis=1)
        query_pos = block_start + jnp.arange(block_rows, dtype=jnp.int32)
        key_pos = block_start - FIRST_WINDOW + jnp.arange(block_rows + FIRST_WINDOW, dtype=jnp.int32)
        return attend_block(query_rows, first_rows, first_vals, second_win, second_vwin, query_pos, key_pos)

    block_list = lax.map(one_block, jnp.arange(token_count // block_rows, dtype=jnp.int32))
    attended = block_list.reshape(token_count, KEY_VALUE_HEADS * GROUP_QUERIES * HEAD_SIZE)
    projected = jnp.dot(attended, out_weight, preferred_element_type=jnp.float32).astype(jnp.bfloat16)
    return attended, projected
```

```python
import math

import jax
import jax.numpy as jnp
from jax import lax
from jax.experimental import pallas as pl
from jax.experimental.pallas import tpu as pltpu
from jax.sharding import PartitionSpec as P

HEAD_SIZE = 128
GROUP_QUERIES = 2
FIRST_WINDOW = 512
SECOND_WINDOW = 32
SUB = 32
OFFSETS = 8
NEG = -1e30
EXP2_SCALE = HEAD_SIZE ** (-0.5) * math.log2(math.e)


def passed_along(x, axis, by):
    size = lax.axis_size(axis)
    pairs = [(i, i + by) for i in range(size) if 0 <= i + by < size]
    return lax.ppermute(x, axis, pairs)


def attend_kernel(first_ref, q_ref, k_ref, v_ref, k2_ref, v2_ref, out_ref, s_ref, m_ref):
    b = pl.program_id(1)
    base = pl.multiple_of(b * SUB, SUB)
    query_first = first_ref[0] + base
    rows_t = GROUP_QUERIES * SUB
    rows = OFFSETS * rows_t
    q = [
        q_ref[:, g * HEAD_SIZE : (g + 1) * HEAD_SIZE].astype(jnp.float32)
        for g in range(GROUP_QUERIES)
    ]
    key_pos = query_first - FIRST_WINDOW + lax.broadcasted_iota(jnp.int32, (1, FIRST_WINDOW), 1)
    bias = jnp.where(key_pos >= 0, 0.0, NEG).astype(jnp.float32)
    lane = lax.broadcasted_iota(jnp.int32, (rows, 128), 1)
    token = lax.rem(lax.broadcasted_iota(jnp.int32, (rows, 128), 0), SUB)
    is_new = lane <= token
    contract = (((1,), (1,)), ((), ()))

    def near(ref, t):
        return ref[pl.ds(base + SECOND_WINDOW - t, SUB), :]

    def fold(s, top):
        s4 = s.reshape(OFFSETS, rows_t, FIRST_WINDOW)
        for tt in range(OFFSETS):
            for c in range(FIRST_WINDOW // 128):
                top = jnp.maximum(top, s4[tt, :, c * 128 : (c + 1) * 128])
        return top

    def scores_step(c, top):
        parts = []
        for tt in range(OFFSETS):
            k2 = near(k2_ref, c * OFFSETS + tt)
            for g in range(GROUP_QUERIES):
                parts.append((q[g] * k2).astype(jnp.bfloat16))
        query_mod = jnp.concatenate(parts, axis=0)
        old = lax.dot_general(
            query_mod,
            k_ref[pl.ds(base, FIRST_WINDOW), :],
            contract,
            preferred_element_type=jnp.float32,
        )
        old = old + bias
        new = lax.dot_general(
            query_mod,
            k_ref[pl.ds(base + FIRST_WINDOW, 128), :],
            contract,
            preferred_element_type=jnp.float32,
        )
        s = jnp.concatenate([jnp.where(is_new, new, old[:, :128]), old[:, 128:]], axis=1)
        s_ref[pl.ds(pl.multiple_of(c * rows, rows), rows), :] = s
        return fold(s, top)

    steps = SECOND_WINDOW // OFFSETS
    low = jnp.full((rows_t, 128), NEG, jnp.float32)
    m_ref[...] = lax.fori_loop(0, steps, scores_step, low)

    @pl.when(query_first < SECOND_WINDOW)
    def _():
        def mask_step(c, top):
            at = pl.ds(pl.multiple_of(c * rows, rows), rows)
            row = lax.broadcasted_iota(jnp.int32, (rows, FIRST_WINDOW), 0)
            offset = c * OFFSETS + row // rows_t
            ok = query_first + lax.rem(row, SUB) - offset >= 0
            s = jnp.where(ok, s_ref[at, :], NEG)
            s_ref[at, :] = s
            return fold(s, top)

        m_ref[...] = lax.fori_loop(0, steps, mask_step, low)

    shift = jnp.max(m_ref[...], axis=1, keepdims=True) * EXP2_SCALE
    shift = jnp.broadcast_to(shift, (rows_t, 128))
    shift_all = jnp.concatenate([shift] * (FIRST_WINDOW // 128), axis=1)
    ones = jnp.ones((FIRST_WINDOW, HEAD_SIZE), jnp.bfloat16)

    def mix_step(c, carry):
        total, weight = carry
        s = s_ref[pl.ds(pl.multiple_of(c * rows, rows), rows), :]
        s = s.reshape(OFFSETS, rows_t, FIRST_WINDOW) * EXP2_SCALE - shift_all[None]
        p = jnp.exp2(s).reshape(rows, FIRST_WINDOW)
        p_old = jnp.concatenate(
            [jnp.where(is_new, 0.0, p[:, :128]).astype(jnp.bfloat16), p[:, 128:].astype(jnp.bfloat16)],
            axis=1,
        )
        p_new = jnp.where(is_new, p[:, :128], 0.0).astype(jnp.bfloat16)
        v_old = jnp.concatenate([v_ref[pl.ds(base, FIRST_WINDOW), :], ones], axis=1)
        v_new = jnp.concatenate([v_ref[pl.ds(base + FIRST_WINDOW, 128), :], ones[:128]], axis=1)
        mix = jnp.dot(p_old, v_old, preferred_element_type=jnp.float32) + jnp.dot(
            p_new, v_new, preferred_element_type=jnp.float32
        )
        for tt in range(OFFSETS):
            v2 = near(v2_ref, c * OFFSETS + tt)
            v2 = jnp.concatenate([v2] * GROUP_QUERIES, axis=0)
            part = mix[tt * rows_t : (tt + 1) * rows_t]
            total = total + part[:, :HEAD_SIZE] * v2
            weight = weight + part[:, HEAD_SIZE:]
        return total, weight

    zero = jnp.zeros((rows_t, HEAD_SIZE), jnp.float32)
    total, weight = lax.fori_loop(0, steps, mix_step, (zero, zero))
    result = (total / weight).astype(jnp.bfloat16)
    for g in range(GROUP_QUERIES):
        out_ref[:, g * HEAD_SIZE : (g + 1) * HEAD_SIZE] = result[g * SUB : (g + 1) * SUB]


def attend(first, queries, keys, values, near_keys, near_values):
    local_rows = queries.shape[0]
    kv_local = keys.shape[1] // HEAD_SIZE
    width = GROUP_QUERIES * HEAD_SIZE
    rows = local_rows * kv_local * GROUP_QUERIES * SECOND_WINDOW

    def whole(x):
        return pl.BlockSpec((x.shape[0], HEAD_SIZE), lambda v, b, first: (0, v))

    block = pl.BlockSpec((SUB, width), lambda v, b, first: (b, v))
    return pl.pallas_call(
        attend_kernel,
        out_shape=jax.ShapeDtypeStruct(queries.shape, jnp.bfloat16),
        grid_spec=pltpu.PrefetchScalarGridSpec(
            num_scalar_prefetch=1,
            grid=(kv_local, local_rows // SUB),
            in_specs=[block, whole(keys), whole(values), whole(near_keys), whole(near_values)],
            out_specs=block,
            scratch_shapes=[
                pltpu.VMEM((SECOND_WINDOW * GROUP_QUERIES * SUB, FIRST_WINDOW), jnp.float32),
                pltpu.VMEM((GROUP_QUERIES * SUB, 128), jnp.float32),
            ],
        ),
        compiler_params=pltpu.CompilerParams(vmem_limit_bytes=40 * 1024 * 1024),
        cost_estimate=pl.CostEstimate(
            flops=rows * 2 * 2 * 768 * 256, bytes_accessed=8 << 20, transcendentals=rows * 512
        ),
    )(first, queries, keys, values, near_keys, near_values)


def on_device(
    queries, first_pair_keys, first_pair_values, second_pair_keys, second_pair_values, out_weight
):
    local_rows, columns = queries.shape
    width = first_pair_keys.shape[1]
    seq_index = lax.axis_index("seq")
    hop_count = FIRST_WINDOW // local_rows
    all_weight = lax.all_gather(out_weight, "seq", axis=0, tiled=True)
    pair = jnp.concatenate([first_pair_keys, first_pair_values], axis=1)
    near = jnp.concatenate([second_pair_keys, second_pair_values], axis=1)
    parts = [passed_along(pair, "seq", hop) for hop in range(hop_count, 0, -1)] + [
        pair,
        jnp.zeros((128, 2 * width), jnp.bfloat16),
    ]
    window = jnp.concatenate(parts, axis=0)
    edge = passed_along(near[local_rows - SECOND_WINDOW :], "seq", 1)
    near = jnp.concatenate([edge, near], axis=0).astype(jnp.float32)
    attended = attend(
        (seq_index * local_rows).astype(jnp.int32)[None],
        queries,
        window[:, :width],
        window[:, width:],
        near[:, :width],
        near[:, width:],
    )
    heads = lax.axis_size("head")
    me = lax.axis_index("head")
    all_heads = jnp.zeros((local_rows, heads * columns), jnp.bfloat16)
    all_heads = lax.dynamic_update_slice(all_heads, attended, (0, me * columns))
    for k in range(1, heads):
        other = lax.ppermute(attended, "head", [(i, (i + k) % heads) for i in range(heads)])
        at = lax.rem(me + heads - k, heads) * columns
        all_heads = lax.dynamic_update_slice(all_heads, other, (0, at))
    projected = jnp.dot(all_heads, all_weight, preferred_element_type=jnp.float32)
    return (attended, projected.astype(jnp.bfloat16))


def solution(mesh):
    spec = P("seq", "head")
    return jax.shard_map(
        on_device, mesh=mesh, in_specs=(spec,) * 6, out_specs=(spec, spec), check_vma=False
    )
```

```python
import math

import jax
import jax.numpy as jnp
from jax import lax
from jax.experimental import pallas as pl
from jax.experimental.pallas import tpu as pltpu
from jax.sharding import PartitionSpec as P

HEAD_SIZE = 128
GROUP_QUERIES = 2
FIRST_WINDOW = 512
SECOND_WINDOW = 32
SUB = 32
OFFSETS = 8
SHARERS = 4
NEG = -1e30
EXP2_SCALE = HEAD_SIZE ** (-0.5) * math.log2(math.e)


def passed_along(x, axis, by):
    size = lax.axis_size(axis)
    pairs = [(i, i + by) for i in range(size) if 0 <= i + by < size]
    return lax.ppermute(x, axis, pairs)


def attend_kernel(first_ref, q_ref, k_ref, v_ref, k2_ref, v2_ref, out_ref, s_ref, m_ref):
    b = pl.program_id(1)
    base = pl.multiple_of(b * SUB, SUB)
    query_first = first_ref[0] + base
    rows_t = GROUP_QUERIES * SUB
    rows = OFFSETS * rows_t
    q = [
        q_ref[:, g * HEAD_SIZE : (g + 1) * HEAD_SIZE].astype(jnp.float32)
        for g in range(GROUP_QUERIES)
    ]
    key_pos = query_first - FIRST_WINDOW + lax.broadcasted_iota(jnp.int32, (1, FIRST_WINDOW), 1)
    bias = jnp.where(key_pos >= 0, 0.0, NEG).astype(jnp.float32)
    lane = lax.broadcasted_iota(jnp.int32, (rows, 128), 1)
    token = lax.rem(lax.broadcasted_iota(jnp.int32, (rows, 128), 0), SUB)
    is_new = lane <= token
    contract = (((1,), (1,)), ((), ()))

    def near(ref, t):
        return ref[pl.ds(base + SECOND_WINDOW - t, SUB), :]

    def fold(s, top):
        s4 = s.reshape(OFFSETS, rows_t, FIRST_WINDOW)
        for tt in range(OFFSETS):
            for c in range(FIRST_WINDOW // 128):
                top = jnp.maximum(top, s4[tt, :, c * 128 : (c + 1) * 128])
        return top

    def scores_step(c, top):
        parts = []
        for tt in range(OFFSETS):
            k2 = near(k2_ref, c * OFFSETS + tt)
            for g in range(GROUP_QUERIES):
                parts.append((q[g] * k2).astype(jnp.bfloat16))
        query_mod = jnp.concatenate(parts, axis=0)
        old = lax.dot_general(
            query_mod,
            k_ref[pl.ds(base, FIRST_WINDOW), :],
            contract,
            preferred_element_type=jnp.float32,
        )
        old = old + bias
        new = lax.dot_general(
            query_mod,
            k_ref[pl.ds(base + FIRST_WINDOW, 128), :],
            contract,
            preferred_element_type=jnp.float32,
        )
        s = jnp.concatenate([jnp.where(is_new, new, old[:, :128]), old[:, 128:]], axis=1)
        s_ref[pl.ds(pl.multiple_of(c * rows, rows), rows), :] = s
        return fold(s, top)

    steps = SECOND_WINDOW // OFFSETS
    low = jnp.full((rows_t, 128), NEG, jnp.float32)
    m_ref[...] = lax.fori_loop(0, steps, scores_step, low)

    @pl.when(query_first < SECOND_WINDOW)
    def _():
        def mask_step(c, top):
            at = pl.ds(pl.multiple_of(c * rows, rows), rows)
            row = lax.broadcasted_iota(jnp.int32, (rows, FIRST_WINDOW), 0)
            offset = c * OFFSETS + row // rows_t
            ok = query_first + lax.rem(row, SUB) - offset >= 0
            s = jnp.where(ok, s_ref[at, :], NEG)
            s_ref[at, :] = s
            return fold(s, top)

        m_ref[...] = lax.fori_loop(0, steps, mask_step, low)

    shift = jnp.max(m_ref[...], axis=1, keepdims=True) * EXP2_SCALE
    shift = jnp.broadcast_to(shift, (rows_t, 128))
    shift_all = jnp.concatenate([shift] * (FIRST_WINDOW // 128), axis=1)
    ones = jnp.ones((FIRST_WINDOW, HEAD_SIZE), jnp.bfloat16)

    def mix_step(c, carry):
        total, weight = carry
        s = s_ref[pl.ds(pl.multiple_of(c * rows, rows), rows), :]
        s = s.reshape(OFFSETS, rows_t, FIRST_WINDOW) * EXP2_SCALE - shift_all[None]
        p = jnp.exp2(s).reshape(rows, FIRST_WINDOW)
        p_old = jnp.concatenate(
            [jnp.where(is_new, 0.0, p[:, :128]).astype(jnp.bfloat16), p[:, 128:].astype(jnp.bfloat16)],
            axis=1,
        )
        p_new = jnp.where(is_new, p[:, :128], 0.0).astype(jnp.bfloat16)
        v_old = jnp.concatenate([v_ref[pl.ds(base, FIRST_WINDOW), :], ones], axis=1)
        v_new = jnp.concatenate([v_ref[pl.ds(base + FIRST_WINDOW, 128), :], ones[:128]], axis=1)
        mix = jnp.dot(p_old, v_old, preferred_element_type=jnp.float32) + jnp.dot(
            p_new, v_new, preferred_element_type=jnp.float32
        )
        for tt in range(OFFSETS):
            v2 = near(v2_ref, c * OFFSETS + tt)
            v2 = jnp.concatenate([v2] * GROUP_QUERIES, axis=0)
            part = mix[tt * rows_t : (tt + 1) * rows_t]
            total = total + part[:, :HEAD_SIZE] * v2
            weight = weight + part[:, HEAD_SIZE:]
        return total, weight

    zero = jnp.zeros((rows_t, HEAD_SIZE), jnp.float32)
    total, weight = lax.fori_loop(0, steps, mix_step, (zero, zero))
    result = (total / weight).astype(jnp.bfloat16)
    for g in range(GROUP_QUERIES):
        out_ref[:, g * HEAD_SIZE : (g + 1) * HEAD_SIZE] = result[g * SUB : (g + 1) * SUB]


def attend(first, split, splits, queries, keys, values, near_keys, near_values):
    local_rows = queries.shape[0]
    kv_part = keys.shape[1] // HEAD_SIZE // splits
    width = GROUP_QUERIES * HEAD_SIZE
    rows = local_rows * kv_part * GROUP_QUERIES * SECOND_WINDOW

    def whole(x):
        return pl.BlockSpec((x.shape[0], HEAD_SIZE), lambda v, b, first: (0, split * kv_part + v))

    return pl.pallas_call(
        attend_kernel,
        out_shape=jax.ShapeDtypeStruct((local_rows, kv_part * width), jnp.bfloat16),
        grid_spec=pltpu.PrefetchScalarGridSpec(
            num_scalar_prefetch=1,
            grid=(kv_part, local_rows // SUB),
            in_specs=[pl.BlockSpec((SUB, width), lambda v, b, first: (b, split * kv_part + v))]
            + [whole(x) for x in (keys, values, near_keys, near_values)],
            out_specs=pl.BlockSpec((SUB, width), lambda v, b, first: (b, v)),
            scratch_shapes=[
                pltpu.VMEM((SECOND_WINDOW * GROUP_QUERIES * SUB, FIRST_WINDOW), jnp.float32),
                pltpu.VMEM((GROUP_QUERIES * SUB, 128), jnp.float32),
            ],
        ),
        compiler_params=pltpu.CompilerParams(vmem_limit_bytes=40 * 1024 * 1024),
        cost_estimate=pl.CostEstimate(
            flops=rows * 2 * 2 * 768 * 256, bytes_accessed=8 << 20, transcendentals=rows * 512
        ),
    )(first, queries, keys, values, near_keys, near_values)


def within_group(x, group, by):
    size = lax.axis_size("seq")
    pairs = [(i, i // group * group + (i + by) % group) for i in range(size)]
    return lax.ppermute(x, "seq", pairs)


def on_device(
    queries, first_pair_keys, first_pair_values, second_pair_keys, second_pair_values, out_weight
):
    local_rows, columns = queries.shape
    width = first_pair_keys.shape[1]
    weight_rows, features = out_weight.shape
    seq_size = lax.axis_size("seq")
    seq_index = lax.axis_index("seq")
    heads = lax.axis_size("head")
    me = lax.axis_index("head")
    group = math.gcd(SHARERS, seq_size)
    member = lax.rem(seq_index, group)
    part = features // group

    pair = jnp.concatenate([first_pair_keys, first_pair_values], axis=1)
    near = jnp.concatenate([second_pair_keys, second_pair_values], axis=1)

    share = jnp.zeros((group * weight_rows, part), jnp.bfloat16)
    for k in range(group):
        to = lax.rem(member + k, group)
        piece = lax.dynamic_slice(out_weight, (0, to * part), (weight_rows, part))
        if k:
            piece = within_group(piece, group, k)
        source = lax.rem(member + group - k, group)
        share = lax.dynamic_update_slice(share, piece, (source * weight_rows, 0))
    hop_count = FIRST_WINDOW // local_rows
    parts = [passed_along(pair, "seq", hop) for hop in range(hop_count, 0, -1)] + [
        pair,
        jnp.zeros((128, 2 * width), jnp.bfloat16),
    ]
    window = jnp.concatenate(parts, axis=0)
    edge = passed_along(near[local_rows - SECOND_WINDOW :], "seq", 1)
    near = jnp.concatenate([edge, near], axis=0).astype(jnp.float32)
    share, queries = lax.optimization_barrier((share, queries))
    my_weight = lax.all_gather(
        share,
        "seq",
        axis=0,
        tiled=True,
        axis_index_groups=[list(range(p, seq_size, group)) for p in range(group)],
    )

    splits = math.gcd(2, width // HEAD_SIZE)
    split_columns = columns // splits
    all_heads = jnp.zeros((group * local_rows, heads * columns), jnp.bfloat16)
    attended = []
    for split in range(splits):
        mine = attend(
            (seq_index * local_rows).astype(jnp.int32)[None],
            split,
            splits,
            queries,
            window[:, :width],
            window[:, width:],
            near[:, :width],
            near[:, width:],
        )
        attended.append(mine)
        tokens = jnp.concatenate(
            [mine] + [within_group(mine, group, k) for k in range(1, group)], axis=0
        )
        for k in range(heads):
            other = tokens
            if k:
                other = lax.ppermute(tokens, "head", [(i, (i + k) % heads) for i in range(heads)])
            at = lax.rem(me + heads - k, heads) * columns + split * split_columns
            all_heads = lax.dynamic_update_slice(all_heads, other, (0, at))
    attended = jnp.concatenate(attended, axis=1)

    projected = jnp.zeros((local_rows, features), jnp.bfloat16)
    for k in list(range(1, group)) + [0]:
        block = jnp.dot(
            all_heads[k * local_rows : (k + 1) * local_rows],
            my_weight,
            preferred_element_type=jnp.float32,
        ).astype(jnp.bfloat16)
        if k:
            block = within_group(block, group, group - k)
        projected = lax.dynamic_update_slice(
            projected, block, (0, lax.rem(member + k, group) * part)
        )
    return (attended, projected)


def solution(mesh):
    spec = P("seq", "head")
    return jax.shard_map(
        on_device, mesh=mesh, in_specs=(spec,) * 6, out_specs=(spec, spec), check_vma=False
    )
```

```python
import math

import jax
import jax.numpy as jnp
from jax import lax
from jax.experimental import pallas as pl
from jax.experimental.pallas import tpu as pltpu
from jax.sharding import PartitionSpec as P

HEAD_SIZE = 128
GROUP_QUERIES = 2
FIRST_WINDOW = 512
SECOND_WINDOW = 32
SUB = 32
OFFSETS = 8
SHARERS = 4
NEG = -1e30
EXP2_SCALE = HEAD_SIZE ** (-0.5) * math.log2(math.e)


def passed_along(x, axis, by):
    size = lax.axis_size(axis)
    pairs = [(i, i + by) for i in range(size) if 0 <= i + by < size]
    return lax.ppermute(x, axis, pairs)


def attend_kernel(first_ref, q_ref, k_ref, v_ref, k2_ref, v2_ref, out_ref, s_ref, m_ref):
    b = pl.program_id(1)
    base = pl.multiple_of(b * SUB, SUB)
    query_first = first_ref[0] + base
    rows_t = GROUP_QUERIES * SUB
    rows = OFFSETS * rows_t
    q = [
        q_ref[:, g * HEAD_SIZE : (g + 1) * HEAD_SIZE].astype(jnp.float32)
        for g in range(GROUP_QUERIES)
    ]
    key_pos = query_first - FIRST_WINDOW + lax.broadcasted_iota(jnp.int32, (1, FIRST_WINDOW), 1)
    bias = jnp.where(key_pos >= 0, 0.0, NEG).astype(jnp.float32)
    lane = lax.broadcasted_iota(jnp.int32, (rows, 128), 1)
    token = lax.rem(lax.broadcasted_iota(jnp.int32, (rows, 128), 0), SUB)
    is_new = lane <= token
    contract = (((1,), (1,)), ((), ()))

    def near(ref, t):
        return ref[pl.ds(base + SECOND_WINDOW - t, SUB), :]

    def fold(s, top):
        s4 = s.reshape(OFFSETS, rows_t, FIRST_WINDOW)
        for tt in range(OFFSETS):
            for c in range(FIRST_WINDOW // 128):
                top = jnp.maximum(top, s4[tt, :, c * 128 : (c + 1) * 128])
        return top

    def scores_step(c, top):
        parts = []
        for tt in range(OFFSETS):
            k2 = near(k2_ref, c * OFFSETS + tt)
            for g in range(GROUP_QUERIES):
                parts.append((q[g] * k2).astype(jnp.bfloat16))
        query_mod = jnp.concatenate(parts, axis=0)
        old = lax.dot_general(
            query_mod,
            k_ref[pl.ds(base, FIRST_WINDOW), :],
            contract,
            preferred_element_type=jnp.float32,
        )
        old = old + bias
        new = lax.dot_general(
            query_mod,
            k_ref[pl.ds(base + FIRST_WINDOW, 128), :],
            contract,
            preferred_element_type=jnp.float32,
        )
        s = jnp.concatenate([jnp.where(is_new, new, old[:, :128]), old[:, 128:]], axis=1)
        s_ref[pl.ds(pl.multiple_of(c * rows, rows), rows), :] = s
        return fold(s, top)

    steps = SECOND_WINDOW // OFFSETS
    low = jnp.full((rows_t, 128), NEG, jnp.float32)
    m_ref[...] = lax.fori_loop(0, steps, scores_step, low)

    @pl.when(query_first < SECOND_WINDOW)
    def _():
        def mask_step(c, top):
            at = pl.ds(pl.multiple_of(c * rows, rows), rows)
            row = lax.broadcasted_iota(jnp.int32, (rows, FIRST_WINDOW), 0)
            offset = c * OFFSETS + row // rows_t
            ok = query_first + lax.rem(row, SUB) - offset >= 0
            s = jnp.where(ok, s_ref[at, :], NEG)
            s_ref[at, :] = s
            return fold(s, top)

        m_ref[...] = lax.fori_loop(0, steps, mask_step, low)

    shift = jnp.max(m_ref[...], axis=1, keepdims=True) * EXP2_SCALE
    shift = jnp.broadcast_to(shift, (rows_t, 128))
    shift_all = jnp.concatenate([shift] * (FIRST_WINDOW // 128), axis=1)
    ones = jnp.ones((FIRST_WINDOW, HEAD_SIZE), jnp.bfloat16)

    def mix_step(c, carry):
        total, weight = carry
        s = s_ref[pl.ds(pl.multiple_of(c * rows, rows), rows), :]
        s = s.reshape(OFFSETS, rows_t, FIRST_WINDOW) * EXP2_SCALE - shift_all[None]
        p = jnp.exp2(s).reshape(rows, FIRST_WINDOW)
        p_old = jnp.concatenate(
            [jnp.where(is_new, 0.0, p[:, :128]).astype(jnp.bfloat16), p[:, 128:].astype(jnp.bfloat16)],
            axis=1,
        )
        p_new = jnp.where(is_new, p[:, :128], 0.0).astype(jnp.bfloat16)
        v_old = jnp.concatenate([v_ref[pl.ds(base, FIRST_WINDOW), :], ones], axis=1)
        v_new = jnp.concatenate([v_ref[pl.ds(base + FIRST_WINDOW, 128), :], ones[:128]], axis=1)
        mix = jnp.dot(p_old, v_old, preferred_element_type=jnp.float32) + jnp.dot(
            p_new, v_new, preferred_element_type=jnp.float32
        )
        for tt in range(OFFSETS):
            v2 = near(v2_ref, c * OFFSETS + tt)
            v2 = jnp.concatenate([v2] * GROUP_QUERIES, axis=0)
            part = mix[tt * rows_t : (tt + 1) * rows_t]
            total = total + part[:, :HEAD_SIZE] * v2
            weight = weight + part[:, HEAD_SIZE:]
        return total, weight

    zero = jnp.zeros((rows_t, HEAD_SIZE), jnp.float32)
    total, weight = lax.fori_loop(0, steps, mix_step, (zero, zero))
    result = (total / weight).astype(jnp.bfloat16)
    for g in range(GROUP_QUERIES):
        out_ref[:, g * HEAD_SIZE : (g + 1) * HEAD_SIZE] = result[g * SUB : (g + 1) * SUB]


def attend(first, split, splits, queries, keys, values, near_keys, near_values):
    local_rows = queries.shape[0]
    kv_part = keys.shape[1] // HEAD_SIZE // splits
    width = GROUP_QUERIES * HEAD_SIZE
    rows = local_rows * kv_part * GROUP_QUERIES * SECOND_WINDOW

    def whole(x):
        return pl.BlockSpec((x.shape[0], HEAD_SIZE), lambda v, b, first: (0, split * kv_part + v))

    return pl.pallas_call(
        attend_kernel,
        out_shape=jax.ShapeDtypeStruct((local_rows, kv_part * width), jnp.bfloat16),
        grid_spec=pltpu.PrefetchScalarGridSpec(
            num_scalar_prefetch=1,
            grid=(kv_part, local_rows // SUB),
            in_specs=[pl.BlockSpec((SUB, width), lambda v, b, first: (b, split * kv_part + v))]
            + [whole(x) for x in (keys, values, near_keys, near_values)],
            out_specs=pl.BlockSpec((SUB, width), lambda v, b, first: (b, v)),
            scratch_shapes=[
                pltpu.VMEM((SECOND_WINDOW * GROUP_QUERIES * SUB, FIRST_WINDOW), jnp.float32),
                pltpu.VMEM((GROUP_QUERIES * SUB, 128), jnp.float32),
            ],
        ),
        compiler_params=pltpu.CompilerParams(vmem_limit_bytes=40 * 1024 * 1024),
        cost_estimate=pl.CostEstimate(
            flops=rows * 2 * 2 * 768 * 256, bytes_accessed=8 << 20, transcendentals=rows * 512
        ),
    )(first, queries, keys, values, near_keys, near_values)


def within_group(x, group, by):
    size = lax.axis_size("seq")
    pairs = [(i, i // group * group + (i + by) % group) for i in range(size)]
    return lax.ppermute(x, "seq", pairs)


def on_device(
    queries, first_pair_keys, first_pair_values, second_pair_keys, second_pair_values, out_weight
):
    local_rows, columns = queries.shape
    width = first_pair_keys.shape[1]
    weight_rows, features = out_weight.shape
    seq_size = lax.axis_size("seq")
    seq_index = lax.axis_index("seq")
    heads = lax.axis_size("head")
    me = lax.axis_index("head")
    group = math.gcd(SHARERS, seq_size)
    member = lax.rem(seq_index, group)
    part = features // group

    pair = jnp.concatenate([first_pair_keys, first_pair_values], axis=1)
    near = jnp.concatenate([second_pair_keys, second_pair_values], axis=1)

    share = jnp.zeros((group * weight_rows, part), jnp.bfloat16)
    for k in range(group):
        to = lax.rem(member + k, group)
        piece = lax.dynamic_slice(out_weight, (0, to * part), (weight_rows, part))
        if k:
            piece = within_group(piece, group, k)
        source = lax.rem(member + group - k, group)
        share = lax.dynamic_update_slice(share, piece, (source * weight_rows, 0))
    hop_count = FIRST_WINDOW // local_rows
    parts = [passed_along(pair, "seq", hop) for hop in range(hop_count, 0, -1)] + [
        pair,
        jnp.zeros((128, 2 * width), jnp.bfloat16),
    ]
    window = jnp.concatenate(parts, axis=0)
    edge = passed_along(near[local_rows - SECOND_WINDOW :], "seq", 1)
    near = jnp.concatenate([edge, near], axis=0).astype(jnp.float32)
    share, queries = lax.optimization_barrier((share, queries))
    my_weight = lax.all_gather(
        share,
        "seq",
        axis=0,
        tiled=True,
        axis_index_groups=[list(range(p, seq_size, group)) for p in range(group)],
    )

    splits = 1
    split_columns = columns // splits
    all_heads = jnp.zeros((group * local_rows, heads * columns), jnp.bfloat16)
    attended = []
    for split in range(splits):
        mine = attend(
            (seq_index * local_rows).astype(jnp.int32)[None],
            split,
            splits,
            queries,
            window[:, :width],
            window[:, width:],
            near[:, :width],
            near[:, width:],
        )
        attended.append(mine)
        tokens = jnp.concatenate(
            [mine] + [within_group(mine, group, k) for k in range(1, group)], axis=0
        )
        for k in range(heads):
            other = tokens
            if k:
                other = lax.ppermute(tokens, "head", [(i, (i + k) % heads) for i in range(heads)])
            at = lax.rem(me + heads - k, heads) * columns + split * split_columns
            all_heads = lax.dynamic_update_slice(all_heads, other, (0, at))
    attended = jnp.concatenate(attended, axis=1)

    projected = jnp.zeros((local_rows, features), jnp.bfloat16)
    for k in list(range(1, group)) + [0]:
        block = jnp.dot(
            all_heads[k * local_rows : (k + 1) * local_rows],
            my_weight,
            preferred_element_type=jnp.float32,
        ).astype(jnp.bfloat16)
        if k:
            block = within_group(block, group, group - k)
        projected = lax.dynamic_update_slice(
            projected, block, (0, lax.rem(member + k, group) * part)
        )
    return (attended, projected)


def solution(mesh):
    spec = P("seq", "head")
    return jax.shard_map(
        on_device, mesh=mesh, in_specs=(spec,) * 6, out_specs=(spec, spec), check_vma=False
    )
```
